128 devices in a mesh: dp: 16 (over x, z), section: 8 (over y, core).
Axes of the slice: x: 4, y: 4, z: 4, core: 2. Of those that a mesh axis runs over, the one named last changes fastest.
Arguments:
- acts: bfloat16 [8, 128, 6144], P('section', None, 'dp'), may hold values from -6 to 6
- grad_top: bfloat16 [128, 6144], P(None, 'dp'), may hold values from -6 to 6
- weights_t: bfloat16 [8, 6144, 6144], P('section', 'dp'), may hold values from -0.078125 to 0.078125
- slopes: bfloat16 [8, 128, 6144], P('section', None, 'dp'), may hold values from 0.19921875 to 1.59375
- running: float32 [8, 24, 512, 512], P('section', None, 'dp'), as said below
- ns_counts: int32 [8, 24], P('section'), may hold values from 1 to 2
- assignment: int32 [8, 24], P('section'), may hold values from 0 to 15, as said below
Outputs:
- backs: bfloat16 [8, 128, 6144], P('section', None, 'dp')
- precond_acts: bfloat16 [8, 128, 6144], P('section', None, 'dp')
- precond_grads: bfloat16 [8, 128, 6144], P('section', None, 'dp')
- inverses: bfloat16 [8, 16, 3, 512, 512], P('section', 'dp')
The draws below stay inside these ranges and needn't reach their ends.
Inputs may be any that keep to these rules, and one draw needn't show every extreme that they name: `assignment`: each tile of a layer names the dp index that owns it. No owner holds more than 3 tiles of one layer, and in every layer one owner holds exactly 3. `running`: every tile is symmetric.
All inputs are finite; a program needn't handle non-finite values. Where the reference program divides by a largest or mean magnitude, that divisor is 1e-20 or more.
Results may differ from the reference program's by a relative error of at most 0.035.
Values may be sent and summed in bfloat16 or wider, within the bound.
A program may use at most 64 MiB of HBM per device.

```python
import jax
import jax.numpy as jnp
from jax import lax

D = 6144
BLOCK = 512
ROWS = 128
MOST = 3
NS_ITERS = 2
SECTIONS = 8
NBLK = 12
TILES = 24
N_DP = 16


def draw_running(key, part):
    key = jax.random.fold_in(key, 5)
    key_a, key_b = jax.random.split(key)
    shape = (SECTIONS, TILES, BLOCK, BLOCK)
    entries = jax.random.truncated_normal(key_a, -4.0, 4.0, shape, jnp.float32)
    diagonal = jnp.exp(jax.random.uniform(key_b, (SECTIONS, TILES, BLOCK), jnp.float32, jnp.log(0.5), jnp.log(5.0)))
    symmetric = (entries + jnp.swapaxes(entries, -1, -2)) * 0.7071
    ident = jnp.eye(BLOCK, dtype=jnp.float32)
    roots = jnp.sqrt(diagonal)
    offdiag = symmetric * (1.0 - ident) * 0.015 * roots[..., :, None] * roots[..., None, :]
    return offdiag + ident * diagonal[..., None]


def draw_assignment(key, part):
    key = jax.random.fold_in(key, 11)

    def one_section(section_key):
        key_a, key_b = jax.random.split(section_key)
        ordering = jax.random.permutation(key_a, TILES)
        ranks = jnp.argsort(ordering).astype(jnp.int32)
        owners = jax.random.permutation(key_b, N_DP).astype(jnp.int32)
        groups = jnp.where(ranks < MOST, 0, 1 + (ranks - MOST) % (N_DP - 1))
        return owners[groups].astype(jnp.int32)
    section_keys = jax.random.split(key, SECTIONS)
    return jax.vmap(one_section)(section_keys)


def plant(values, own_key, smallest, high):
    extent = values.shape
    place = [jax.random.randint(jax.random.fold_in(own_key, axis), (), 0, extent[axis]) for axis in range(len(extent))]
    values = values.at[tuple(place)].set(smallest)
    longest = extent.index(max(extent))
    place[longest] = (place[longest] + 1) % extent[longest]
    return values.at[tuple(place)].set(high)


def steps_of(rng, extent, cuts, low, largest):
    level = 1.0
    for axis_at, parts in cuts:
        steps = jax.random.uniform(jax.random.fold_in(jax.random.fold_in(rng, 6), axis_at), (parts,), jnp.float32, low / len(cuts), largest / len(cuts))
        level = level * jnp.repeat(jnp.exp(steps), extent[axis_at] // parts).reshape((-1,) + (1,) * (len(extent) - 1 - axis_at))
    return level


def noise(own_key, dims, width, bound, cuts=(), held_as=jnp.bfloat16):
    array = width * jax.random.normal(own_key, dims, jnp.float32)
    if cuts:
        array = array * steps_of(own_key, dims, cuts, -0.22, 0.18)
    return jnp.clip(array, -bound, bound).astype(held_as)


def setup_inputs(seed: int = 0) -> dict:
    arg_keys = jax.random.split(jax.random.key(seed), 8)
    return {
        "acts": noise(arg_keys[0], (SECTIONS, ROWS, D), 1.0, 6.0, ((0, 8), (2, 16))),
        "grad_top": noise(arg_keys[1], (ROWS, D), 1.0, 6.0, ((1, 16),)),
        "weights_t": noise(arg_keys[2], (SECTIONS, D, D), D ** -0.5, 0.078125, ((0, 8), (1, 16))),
        "slopes": jnp.clip(0.19921875 + 1.3945312 * jax.random.uniform(arg_keys[3], (SECTIONS, ROWS, D), jnp.float32) ** steps_of(arg_keys[3], (SECTIONS, ROWS, D), ((0, 8), (2, 16)), -0.2, 0.2), 0.19921875, 1.59375).astype(jnp.bfloat16),
        "running": draw_running(jax.random.fold_in(arg_keys[7], 71), 0),
        "ns_counts": plant(jax.random.randint(arg_keys[5], (SECTIONS, TILES), 1, NS_ITERS + 1), jax.random.fold_in(arg_keys[5], 1), 1, NS_ITERS).astype(jnp.int32),
        "assignment": draw_assignment(jax.random.fold_in(arg_keys[7], 71), 0),
    }


DECAY = 0.8
DAMP = 0.1


def to_bfloat(values):
    return lax.optimization_barrier(values.astype(jnp.bfloat16)).astype(jnp.float32)


def chain_backward(grad_top, weights_t, slopes):
    width_group = D // N_DP
    backs = [None] * SECTIONS
    out_grads = [None] * SECTIONS
    gradient = grad_top
    for s in range(SECTIONS - 1, -1, -1):
        out_grads[s] = gradient
        pieces = gradient.reshape(ROWS, N_DP, width_group).astype(jnp.float32)
        weight_rows = weights_t[s].reshape(N_DP, width_group, D).astype(jnp.float32)
        summands = jnp.einsum("rkg,kgd->krd", pieces, weight_rows, precision=lax.Precision.HIGHEST)
        summed = jnp.sum(to_bfloat(summands), axis=0)
        backward = (summed * slopes[s].astype(jnp.float32)).astype(jnp.bfloat16)
        backs[s] = backward
        gradient = backward
    return backs, out_grads


def newton(factor, step_counts):
    ident = jnp.eye(BLOCK, dtype=jnp.float32)
    scales = jnp.max(jnp.sum(jnp.abs(factor), axis=2), axis=1)[:, None, None]
    iterate = (2.0 * ident - factor / scales) / scales
    factor_b = to_bfloat(factor)
    for k in range(1, NS_ITERS):
        iterate_b = to_bfloat(iterate)
        product = jnp.einsum("tij,tjk->tik", factor_b, iterate_b, precision=lax.Precision.HIGHEST)
        remainder = to_bfloat(2.0 * ident - product)
        advanced = jnp.einsum("tij,tjk->tik", iterate_b, remainder, precision=lax.Precision.HIGHEST)
        iterate = jnp.where((step_counts > k)[:, None, None], advanced, iterate)
    return iterate.astype(jnp.bfloat16)


def one_section(acts_s, out_grad, running_s, counts_s, owners):
    tiles_x = jnp.concatenate([acts_s.reshape(ROWS, NBLK, BLOCK).transpose(1, 0, 2),
                               out_grad.reshape(ROWS, NBLK, BLOCK).transpose(1, 0, 2)], axis=0)
    tiles_f = tiles_x.astype(jnp.float32)
    grams = jnp.einsum("trb,trc->tbc", tiles_f, tiles_f, precision=lax.Precision.HIGHEST)
    factor = DECAY * running_s + (1.0 - DECAY) * (grams / ROWS) + DAMP * jnp.eye(BLOCK, dtype=jnp.float32)
    inverse_b = newton(factor, counts_s)
    inverse_f = lax.optimization_barrier(inverse_b).astype(jnp.float32)
    precond = jnp.einsum("trb,tbc->trc", tiles_f, inverse_f, precision=lax.Precision.HIGHEST).astype(jnp.bfloat16)
    pre_acts = precond[:NBLK].transpose(1, 0, 2).reshape(ROWS, D)
    pre_grads = precond[NBLK:].transpose(1, 0, 2).reshape(ROWS, D)
    tile_ids = jnp.arange(TILES, dtype=jnp.int32)
    matches = (owners[:, None] == owners[None, :]) & (tile_ids[None, :] < tile_ids[:, None])
    slots_of = jnp.sum(matches.astype(jnp.int32), axis=1).astype(jnp.int32)
    held = jnp.zeros((N_DP, MOST, BLOCK, BLOCK), jnp.bfloat16).at[owners, slots_of].set(inverse_b)
    return pre_acts, pre_grads, held


def reference(acts, grad_top, weights_t, slopes, running, ns_counts, assignment):
    backs, out_grads = chain_backward(grad_top, weights_t, slopes)
    results = [one_section(acts[s], out_grads[s], running[s], ns_counts[s], assignment[s]) for s in range(SECTIONS)]
    return (jnp.stack(backs),
            jnp.stack([item[0] for item in results]),
            jnp.stack([item[1] for item in results]),
            jnp.stack([item[2] for item in results]))
```

```python
import jax
import jax.numpy as jnp
from jax import lax
from jax.experimental import pallas as pl
from jax.experimental.pallas import tpu as pltpu
from jax.sharding import PartitionSpec as P

BLOCK = 512
ROWS = 128
MOST = 3
NBLK = 12
TILES = 24
N_DP = 16
SIDE = 4
SECTIONS = 8
WIDTH = 384
CHUNK = 128
PER = WIDTH // CHUNK
GRADS = NBLK * BLOCK // CHUNK
SLICE = BLOCK // N_DP
STRIPE = 64
DECAY = 0.8
DAMP = 0.1
MESH = pl.DeviceIdType.MESH


def kernel(
    table, counts, acts, grad_top, slopes, weights, running,
    backs_o, pre_acts_o, pre_grads_o, inverses_o,
    w_s, run_s, rows_s, outbox, held, xall, inc, parts, terms, acc,
    mat_a, mat_b, fb, xb, rem, inv, pre,
    load_sem, hop_send, hop_recv,
    rs_send, rs_recv, ag_send, ag_recv, ax_send, ax_recv,
    ra_send, ra_recv, rb_send, rb_recv, rc_send, rc_recv,
):
    me = lax.axis_index("dp")
    sec = lax.axis_index("section")
    my_x, my_z = me // SIDE, me % SIDE

    def to(r):
        return ((my_x + r // SIDE) % SIDE) * SIDE + (my_z + r % SIDE) % SIDE

    def source(r):
        return ((my_x + SIDE - r // SIDE) % SIDE) * SIDE + (my_z + SIDE - r % SIDE) % SIDE

    def base_of(d):
        return 3 * (d // 4) + (d % 4) // 2

    w_copy = pltpu.make_async_copy(weights, w_s, load_sem.at[0])
    run_copy = pltpu.make_async_copy(running, run_s, load_sem.at[1])
    w_copy.start()
    run_copy.start()

    barrier = pltpu.get_barrier_semaphore()

    @pl.loop(1, N_DP)
    def _(r):
        pl.semaphore_signal(barrier, inc=1, device_id=(to(r), sec), device_id_type=MESH)

    @pl.when(sec > 0)
    def _():
        pl.semaphore_signal(barrier, inc=1, device_id=(me, sec - 1), device_id_type=MESH)

    @pl.when(sec < SECTIONS - 1)
    def _():
        pl.semaphore_signal(barrier, inc=1, device_id=(me, sec + 1), device_id_type=MESH)

    edge = jnp.where((sec == 0) | (sec == SECTIONS - 1), 1, 0)
    pl.semaphore_wait(barrier, N_DP + 1 - edge)

    def rs_copy(r):
        return pltpu.make_async_remote_copy(
            parts.at[r], terms.at[r], rs_send.at[r], rs_recv.at[r],
            device_id=(to(r), sec), device_id_type=MESH)

    def gather_copy(r, first, send, recv, peer, owner):
        mine = xall.at[pl.ds(first + PER * owner, PER)]
        return pltpu.make_async_remote_copy(
            mine, mine, send.at[r], recv.at[r], device_id=(peer, sec), device_id_type=MESH)

    def ax_copy(r, owner):
        return gather_copy(r, 0, ax_send, ax_recv, to(r), owner)

    def ag_copy(r, owner):
        return gather_copy(r, GRADS, ag_send, ag_recv, to(r), owner)

    def ra_copy(r, owner):
        peer = to(r)
        return pltpu.make_async_remote_copy(
            outbox.at[pl.ds(MOST * peer, MOST)],
            held.at[pl.ds(4, MOST), pl.ds(pl.multiple_of(SLICE * owner, SLICE), SLICE)],
            ra_send.at[r], ra_recv.at[r], device_id=(peer, sec), device_id_type=MESH)

    def rb_copy(r, owner):
        peer = to(r)
        return pltpu.make_async_remote_copy(
            rows_s.at[pl.ds(base_of(peer), 2)],
            held.at[pl.ds(0, 2), pl.ds(pl.multiple_of(SLICE * owner, SLICE), SLICE)],
            rb_send.at[r], rb_recv.at[r], device_id=(peer, sec), device_id_type=MESH)

    def rc_copy(r, owner):
        peer = to(r)
        return pltpu.make_async_remote_copy(
            rows_s.at[pl.ds(NBLK + base_of(peer), 2)],
            held.at[pl.ds(2, 2), pl.ds(pl.multiple_of(SLICE * owner, SLICE), SLICE)],
            rc_send.at[r], rc_recv.at[r], device_id=(peer, sec), device_id_type=MESH)

    def redistribute():
        run_copy.wait()
        for i in range(PER):
            xall[PER * me + i] = acts[:, i * CHUNK:(i + 1) * CHUNK]

        @pl.loop(1, N_DP)
        def _(r):
            ax_copy(r, me).start()

        @pl.loop(0, TILES)
        def _(t):
            rows_s[t] = run_s[t].astype(jnp.bfloat16)

        @pl.loop(1, N_DP)
        def _(r):
            rb_copy(r, me).start()
            rc_copy(r, me).start()

        @pl.loop(0, N_DP * MOST)
        def _(q):
            outbox[q] = rows_s[jnp.maximum(table[q], 0)]

        @pl.loop(1, N_DP)
        def _(r):
            ra_copy(r, me).start()

        own = pl.ds(pl.multiple_of(SLICE * me, SLICE), SLICE)
        for k in range(2):
            held[k, own] = rows_s[base_of(me) + k]
            held[2 + k, own] = rows_s[NBLK + base_of(me) + k]
        for m in range(MOST):
            held[4 + m, own] = outbox[MOST * me + m]

    pl.when(sec < SECTIONS // 2)(redistribute)

    hop = pltpu.make_async_remote_copy(
        backs_o, inc, hop_send, hop_recv, device_id=(me, jnp.maximum(sec - 1, 0)), device_id_type=MESH)

    @pl.when(sec == SECTIONS - 1)
    def _():
        inc[...] = grad_top[...]

    @pl.when(sec < SECTIONS - 1)
    def _():
        hop.wait_recv()

    for i in range(PER):
        xall[GRADS + PER * me + i] = inc[:, i * CHUNK:(i + 1) * CHUNK]

    def gather_grads():
        @pl.loop(1, N_DP)
        def _(r):
            ag_copy(r, me).start()

    pl.when(sec == 0)(gather_grads)
    w_copy.wait()

    def part(r):
        columns = pl.ds(pl.multiple_of(WIDTH * to(r), CHUNK), WIDTH)
        return jnp.dot(inc[...], w_s[:, columns], preferred_element_type=jnp.float32).astype(jnp.bfloat16)

    @pl.loop(1, N_DP)
    def _(r):
        parts[r] = part(r)
        rs_copy(r).start()

    acc[...] = part(0).astype(jnp.float32)
    pl.when(sec > 0)(gather_grads)

    @pl.loop(1, N_DP)
    def _(r):
        rs_copy(r).wait_recv()
        acc[...] += terms[r].astype(jnp.float32)

    backs_o[...] = (acc[...] * slopes[...].astype(jnp.float32)).astype(jnp.bfloat16)

    @pl.when(sec > 0)
    def _():
        hop.start()

    pl.when(sec >= SECTIONS // 2)(redistribute)

    def diagonal(at):
        row = lax.broadcasted_iota(jnp.int32, (STRIPE, BLOCK), 0) + at * STRIPE
        return row == lax.broadcasted_iota(jnp.int32, (STRIPE, BLOCK), 1)

    def tile(i, owned):
        if owned:
            entry = table[MOST * me + i - 4]
            which = jnp.maximum(entry, 0)
        else:
            which = base_of(me) + jnp.where(i < 2, i, NBLK - 2 + i)
        x = jnp.concatenate([xall[4 * which + k] for k in range(4)], axis=1)
        mat_a[...] = lax.dot_general(x, x, (((0,), (0,)), ((), ())), preferred_element_type=jnp.float32)
        total = jnp.zeros((8, BLOCK), jnp.float32)
        for at in range(BLOCK // STRIPE):
            rows = pl.ds(at * STRIPE, STRIPE)
            value = DECAY * held[i, rows].astype(jnp.float32) + ((1.0 - DECAY) / ROWS) * mat_a[rows]
            value = value + jnp.where(diagonal(at), DAMP, 0.0)
            mat_a[rows] = value
            fb[rows] = value.astype(jnp.bfloat16)
            total = total + jnp.sum(jnp.abs(value).reshape(STRIPE // 8, 8, BLOCK), axis=0)
        scale = jnp.max(jnp.sum(total, axis=0, keepdims=True), axis=1, keepdims=True)
        recip = 1.0 / scale
        for at in range(BLOCK // STRIPE):
            rows = pl.ds(at * STRIPE, STRIPE)
            xb[rows] = ((jnp.where(diagonal(at), 2.0, 0.0) - mat_a[rows] * recip) * recip).astype(jnp.bfloat16)
        mat_b[...] = jnp.dot(fb[...], xb[...], preferred_element_type=jnp.float32)
        for at in range(BLOCK // STRIPE):
            rows = pl.ds(at * STRIPE, STRIPE)
            rem[rows] = (jnp.where(diagonal(at), 2.0, 0.0) - mat_b[rows]).astype(jnp.bfloat16)
        mat_b[...] = jnp.dot(xb[...], rem[...], preferred_element_type=jnp.float32)
        twice = counts[which] > 1
        for at in range(BLOCK // STRIPE):
            rows = pl.ds(at * STRIPE, STRIPE)
            inv[rows] = jnp.where(twice, mat_b[rows], xb[rows].astype(jnp.float32)).astype(jnp.bfloat16)

        if owned:
            inverses_o[i - 4] = jnp.where(entry >= 0, inv[...].astype(jnp.float32), 0.0).astype(jnp.bfloat16)
        else:
            pre[i] = jnp.dot(x, inv[...], preferred_element_type=jnp.float32).astype(jnp.bfloat16)

    def columns_out(out, first):
        start = 3 * me - 4 * base_of(me)
        for i in range(PER):
            at = start + i
            lane = pl.ds(pl.multiple_of((at % 4) * CHUNK, CHUNK), CHUNK)
            out[:, i * CHUNK:(i + 1) * CHUNK] = pre[first + at // 4, :, lane]

    @pl.loop(1, N_DP)
    def _(r):
        ax_copy(r, source(r)).wait_recv()
        rb_copy(r, source(r)).wait_recv()

    @pl.loop(0, 2)
    def _(i):
        tile(i, False)

    columns_out(pre_acts_o, 0)

    @pl.loop(1, N_DP)
    def _(r):
        ag_copy(r, source(r)).wait_recv()
        rc_copy(r, source(r)).wait_recv()
        ra_copy(r, source(r)).wait_recv()

    @pl.loop(2, 4)
    def _(i):
        tile(i, False)

    columns_out(pre_grads_o, 2)

    @pl.loop(4, 4 + MOST)
    def _(i):
        tile(i, True)

    @pl.loop(1, N_DP)
    def _(r):
        rs_copy(r).wait_send()
        ax_copy(r, me).wait_send()
        ag_copy(r, me).wait_send()
        ra_copy(r, me).wait_send()
        rb_copy(r, me).wait_send()
        rc_copy(r, me).wait_send()

    @pl.when(sec > 0)
    def _():
        hop.wait_send()


def shards(acts, grad_top, weights_t, slopes, running, ns_counts, assignment):
    owners = assignment[0]
    tile_ids = jnp.arange(TILES, dtype=jnp.int32)
    matches = (owners[:, None] == owners[None, :]) & (tile_ids[None, :] < tile_ids[:, None])
    slots_of = jnp.sum(matches.astype(jnp.int32), axis=1)
    places = jnp.arange(N_DP * MOST, dtype=jnp.int32)
    taken = (owners * MOST + slots_of)[None, :] == places[:, None]
    table = jnp.sum(jnp.where(taken, tile_ids[None, :] + 1, 0), axis=1) - 1
    vmem = pl.BlockSpec(memory_space=pltpu.VMEM)
    smem = pl.BlockSpec(memory_space=pltpu.SMEM)
    hbm = pl.BlockSpec(memory_space=pl.ANY)
    bf16, f32 = jnp.bfloat16, jnp.float32
    flat = jax.ShapeDtypeStruct((ROWS, WIDTH), bf16)
    dma = pltpu.SemaphoreType.DMA
    backs, pre_acts, pre_grads, inverses = pl.pallas_call(
        kernel,
        out_shape=(flat, flat, flat, jax.ShapeDtypeStruct((MOST, BLOCK, BLOCK), bf16)),
        in_specs=[smem, smem, vmem, vmem, vmem, hbm, hbm],
        out_specs=(vmem, vmem, vmem, vmem),
        scratch_shapes=[
            pltpu.VMEM((WIDTH, NBLK * BLOCK), bf16),
            pltpu.VMEM((TILES, SLICE, BLOCK), f32),
            pltpu.VMEM((TILES, SLICE, BLOCK), bf16),
            pltpu.VMEM((N_DP * MOST, SLICE, BLOCK), bf16),
            pltpu.VMEM((4 + MOST, BLOCK, BLOCK), bf16),
            pltpu.VMEM((2 * GRADS, ROWS, CHUNK), bf16),
            pltpu.VMEM((ROWS, WIDTH), bf16),
            pltpu.VMEM((N_DP, ROWS, WIDTH), bf16),
            pltpu.VMEM((N_DP, ROWS, WIDTH), bf16),
            pltpu.VMEM((ROWS, WIDTH), f32),
            pltpu.VMEM((BLOCK, BLOCK), f32),
            pltpu.VMEM((BLOCK, BLOCK), f32),
            pltpu.VMEM((BLOCK, BLOCK), bf16),
            pltpu.VMEM((BLOCK, BLOCK), bf16),
            pltpu.VMEM((BLOCK, BLOCK), bf16),
            pltpu.VMEM((BLOCK, BLOCK), bf16),
            pltpu.VMEM((4, ROWS, BLOCK), bf16),
            dma((2,)), dma, dma,
        ] + [dma((N_DP,))] * 12,
        compiler_params=pltpu.CompilerParams(
            collective_id=0, has_side_effects=True, vmem_limit_bytes=48 * 1024 * 1024),
        name="refresh",
    )(table, ns_counts[0], acts[0], grad_top, slopes[0], weights_t[0], running[0])
    return (backs[None], pre_acts[None], pre_grads[None], inverses[None, None])


def solution(mesh):
    in_specs = (
        P("section", None, "dp"),
        P(None, "dp"),
        P("section", "dp", None),
        P("section", None, "dp"),
        P("section", None, "dp", None),
        P("section", None),
        P("section", None),
    )
    out_specs = (
        P("section", None, "dp"),
        P("section", None, "dp"),
        P("section", None, "dp"),
        P("section", "dp", None, None, None),
    )
    return jax.shard_map(shards, mesh=mesh, in_specs=in_specs, out_specs=out_specs, check_vma=False)
```

```python
import jax
import jax.numpy as jnp
from jax import lax
from jax.experimental import pallas as pl
from jax.experimental.pallas import tpu as pltpu
from jax.sharding import PartitionSpec as P

BLOCK = 512
ROWS = 128
MOST = 3
NBLK = 12
TILES = 24
N_DP = 16
SIDE = 4
SECTIONS = 8
WIDTH = 384
CHUNK = 128
PER = WIDTH // CHUNK
CHUNKS = 2 * NBLK * BLOCK // CHUNK
SLICE = BLOCK // N_DP
GROUP = 16
PLACES = N_DP * MOST
STRIPE = 64
PARTS = 4
LOT = ROWS // PARTS
DECAY = 0.8
DAMP = 0.1
MESH = pl.DeviceIdType.MESH
BF16 = jnp.bfloat16
F32 = jnp.float32


def far_first(k):
    return jnp.where(k == 0, 2, jnp.where(k == 1, 1, jnp.where(k == 2, 3, 0)))


def kernel(
    table, place, counts, acts, grad_top, slopes, weights, running,
    backs_o, pre_acts_o, pre_grads_o, inverses_o,
    w_s, run_s, acts_s, slopes_s, rows_s, outbox, held,
    inc, parts, terms, own_x, xrow, fbox, xs, pbox, prcv, prow, pin,
    mat_a, mat_b, fb, xb, rem, inv,
    w_sem, load_sem, hop_send, hop_recv, rs_send, rs_recv, pause,
    ra_send, ra_recv, fa_send, fa_recv, fg_send, fg_recv,
    f2_send, f2_recv, b1_send, b1_recv, b2_send, b2_recv,
):
    me = lax.axis_index("dp")
    sec = lax.axis_index("section")
    my_x, my_z = me // SIDE, me % SIDE
    my_group, my_half = me // 2, me % 2

    def to(r):
        return ((my_x + r // SIDE) % SIDE) * SIDE + (my_z + r % SIDE) % SIDE

    def source(r):
        return ((my_x + SIDE - r // SIDE) % SIDE) * SIDE + (my_z + SIDE - r % SIDE) % SIDE

    def remote(src, dst, send, recv, peer):
        return pltpu.make_async_remote_copy(
            src, dst, send, recv, device_id=(peer, sec), device_id_type=MESH)

    def each_peer(body):
        @pl.loop(0, N_DP - 1)
        def _(k):
            body(far_first(k // SIDE) * SIDE + far_first(k % SIDE))

    def w_copy(x):
        columns = pl.ds(pl.multiple_of(x * (SIDE * WIDTH), CHUNK), SIDE * WIDTH)
        return pltpu.make_async_copy(weights.at[:, columns], w_s.at[:, columns], w_sem.at[x])

    run_copy = pltpu.make_async_copy(running, run_s, load_sem.at[0])
    acts_copy = pltpu.make_async_copy(acts, acts_s, load_sem.at[1])
    slopes_copy = pltpu.make_async_copy(slopes, slopes_s, load_sem.at[2])
    top_copy = pltpu.make_async_copy(grad_top, inc, load_sem.at[3])

    @pl.when(sec == SECTIONS - 1)
    def _():
        top_copy.start()

    for k in (2, 1, 3, 0):
        w_copy((my_x + k) % SIDE).start()
    slopes_copy.start()
    acts_copy.start()
    run_copy.start()

    barrier = pltpu.get_barrier_semaphore()
    each_peer(lambda r: pl.semaphore_signal(barrier, inc=1, device_id=(to(r), sec), device_id_type=MESH))

    @pl.when(sec > 0)
    def _():
        pl.semaphore_signal(barrier, inc=1, device_id=(me, sec - 1), device_id_type=MESH)

    @pl.when(sec < SECTIONS - 1)
    def _():
        pl.semaphore_signal(barrier, inc=1, device_id=(me, sec + 1), device_id_type=MESH)

    edge = jnp.where((sec == 0) | (sec == SECTIONS - 1), 1, 0)
    pl.semaphore_wait(barrier, N_DP + 1 - edge)

    def group_rows(d):
        return pl.ds(pl.multiple_of(GROUP * (d // 2), GROUP), GROUP)

    def ra_copy(r, owner):
        return remote(
            outbox.at[pl.ds(MOST * to(r), MOST)],
            held.at[:, pl.ds(pl.multiple_of(SLICE * owner, SLICE), SLICE)],
            ra_send.at[r], ra_recv.at[r], to(r))

    def fa_copy(r, owner):
        return remote(
            own_x.at[pl.ds(0, PER), group_rows(to(r))], xrow.at[pl.ds(PER * owner, PER)],
            fa_send.at[r], fa_recv.at[r], to(r))

    def fg_copy(r, owner):
        return remote(
            own_x.at[pl.ds(PER, PER), group_rows(to(r))], xrow.at[pl.ds(CHUNKS // 2 + PER * owner, PER)],
            fg_send.at[r], fg_recv.at[r], to(r))

    def f2_copy(r, owner):
        return remote(
            fbox.at[pl.ds(MOST * to(r), MOST)], xs.at[:, owner % 2, :, group_rows(owner)],
            f2_send.at[r], f2_recv.at[r], to(r))

    def b1_copy(r, owner):
        peer = to(r)
        return remote(
            pbox.at[:, peer % 2, :, group_rows(peer)], prcv.at[pl.ds(MOST * owner, MOST)],
            b1_send.at[r], b1_recv.at[r], peer)

    def pair_of(f, half):
        k = f % 4
        return 3 * (f // 4) + jnp.where(k == 0, 0, jnp.where(k == 3, 2, k - half))

    def b2_copy(r, owner):
        return remote(
            prow.at[pair_of(to(r), my_half)], pin.at[owner % 2, :, :, group_rows(owner)],
            b2_send.at[r], b2_recv.at[r], to(r))

    def prepare():
        acts_copy.wait()
        for i in range(PER):
            own_x[i] = acts_s[:, i * CHUNK:(i + 1) * CHUNK]
        each_peer(lambda r: fa_copy(r, me).start())
        xrow[pl.ds(PER * me, PER)] = own_x[pl.ds(0, PER), group_rows(me)]
        run_copy.wait()

        @pl.loop(0, TILES)
        def _(t):
            rows_s[t] = run_s[t].astype(BF16)

        @pl.loop(0, PLACES)
        def _(q):
            outbox[q] = rows_s[jnp.maximum(table[q], 0)]

        each_peer(lambda r: ra_copy(r, me).start())
        held[:, pl.ds(pl.multiple_of(SLICE * me, SLICE), SLICE)] = outbox[pl.ds(MOST * me, MOST)]

    pl.when(sec < SECTIONS - 2)(prepare)

    @pl.when(sec == SECTIONS - 1)
    def _():
        top_copy.wait()

    def lot(m):
        return pl.ds(pl.multiple_of(LOT * m, LOT), LOT)

    def hop(m):
        return pltpu.make_async_remote_copy(
            backs_o.at[lot(m)], inc.at[lot(m)], hop_send.at[m], hop_recv.at[m],
            device_id=(me, jnp.maximum(sec - 1, 0)), device_id_type=MESH)

    def rs_copy(m, r):
        return remote(parts.at[m, to(r)], terms.at[m, r], rs_send.at[m, r], rs_recv.at[m, r], to(r))

    def spread_grads():
        for i in range(PER):
            own_x[PER + i] = inc[:, i * CHUNK:(i + 1) * CHUNK]
        each_peer(lambda r: fg_copy(r, me).start())
        xrow[pl.ds(CHUNKS // 2 + PER * me, PER)] = own_x[pl.ds(PER, PER), group_rows(me)]

    @pl.loop(0, PARTS)
    def _(m):
        @pl.when(sec < SECTIONS - 1)
        def _():
            hop(m).wait_recv()

        pl.when((sec < 2) & (m == PARTS - 1))(spread_grads)

        @pl.loop(0, SIDE)
        def _(a):
            x = (my_x + far_first(a)) % SIDE

            @pl.when(m == 0)
            def _():
                w_copy(x).wait()

            columns = pl.ds(pl.multiple_of(x * (SIDE * WIDTH), CHUNK), SIDE * WIDTH)
            product = jnp.dot(inc[lot(m)], w_s[:, columns], preferred_element_type=F32).astype(BF16)
            for z in range(SIDE):
                parts[m, x * SIDE + z] = product[:, z * WIDTH:(z + 1) * WIDTH]

            @pl.loop(0, SIDE)
            def _(b):
                r = far_first(a) * SIDE + far_first(b)

                @pl.when(r > 0)
                def _():
                    rs_copy(m, r).start()

    slopes_copy.wait()

    @pl.loop(0, PARTS)
    def _(m):
        def add(k, total):
            r = far_first(3 - k // SIDE) * SIDE + far_first(3 - k % SIDE)
            rs_copy(m, r).wait_recv()
            return total + terms[m, r].astype(F32)

        total = lax.fori_loop(1, N_DP, add, parts[m, me].astype(F32))
        backs_o[lot(m)] = (total * slopes_s[lot(m)].astype(F32)).astype(BF16)

        @pl.when(sec > 0)
        def _():
            hop(m).start()

    even = sec % 2 == 0

    @pl.when(even & (sec > 0))
    def _():
        pl.semaphore_signal(pause, inc=1, device_id=(me, sec + 1), device_id_type=MESH)

    @pl.when(jnp.logical_not(even) & (sec > 1))
    def _():
        pl.semaphore_wait(pause, 1)

    pl.when(sec >= SECTIONS - 2)(prepare)
    pl.when(sec >= 2)(spread_grads)

    @pl.loop(1, N_DP)
    def _(r):
        fa_copy(r, source(r)).wait_recv()
        fg_copy(r, source(r)).wait_recv()

    @pl.loop(0, PLACES)
    def _(q):
        first = 4 * jnp.maximum(table[q], 0) + 2 * my_half
        fbox[q, 0] = xrow[first]
        fbox[q, 1] = xrow[first + 1]

    each_peer(lambda r: f2_copy(r, me).start())
    for m in range(MOST):
        xs[m, my_half, :, group_rows(me)] = fbox[MOST * me + m]

    @pl.loop(1, N_DP)
    def _(r):
        ra_copy(r, source(r)).wait_recv()
        f2_copy(r, source(r)).wait_recv()

    def diagonal(at):
        row = lax.broadcasted_iota(jnp.int32, (STRIPE, BLOCK), 0) + at * STRIPE
        return row == lax.broadcasted_iota(jnp.int32, (STRIPE, BLOCK), 1)

    @pl.loop(0, MOST)
    def _(m):
        entry = table[MOST * me + m]
        twice = counts[jnp.maximum(entry, 0)] > 1
        x = jnp.concatenate([xs[m, k // 2, k % 2] for k in range(4)], axis=1)
        mat_a[...] = lax.dot_general(x, x, (((0,), (0,)), ((), ())), preferred_element_type=F32)
        total = jnp.zeros((8, BLOCK), F32)
        for at in range(BLOCK // STRIPE):
            rows = pl.ds(at * STRIPE, STRIPE)
            value = DECAY * held[m, rows].astype(F32) + ((1.0 - DECAY) / ROWS) * mat_a[rows]
            value = value + jnp.where(diagonal(at), DAMP, 0.0)
            mat_a[rows] = value
            fb[rows] = value.astype(BF16)
            total = total + jnp.sum(jnp.abs(value).reshape(STRIPE // 8, 8, BLOCK), axis=0)
        scale = jnp.max(jnp.sum(total, axis=0, keepdims=True), axis=1, keepdims=True)
        recip = 1.0 / scale
        for at in range(BLOCK // STRIPE):
            rows = pl.ds(at * STRIPE, STRIPE)
            xb[rows] = ((jnp.where(diagonal(at), 2.0, 0.0) - mat_a[rows] * recip) * recip).astype(BF16)
        mat_b[...] = jnp.dot(fb[...], xb[...], preferred_element_type=F32)
        for at in range(BLOCK // STRIPE):
            rows = pl.ds(at * STRIPE, STRIPE)
            rem[rows] = (jnp.where(diagonal(at), 2.0, 0.0) - mat_b[rows]).astype(BF16)
        mat_b[...] = jnp.dot(xb[...], rem[...], preferred_element_type=F32)
        for at in range(BLOCK // STRIPE):
            rows = pl.ds(at * STRIPE, STRIPE)
            chosen = jnp.where(twice, mat_b[rows], xb[rows].astype(F32))
            inv[rows] = chosen.astype(BF16)
            inverses_o[m, rows] = jnp.where(entry >= 0, chosen, 0.0).astype(BF16)
        result = jnp.dot(x, inv[...], preferred_element_type=F32).astype(BF16)
        for k in range(4):
            pbox[m, k // 2, k % 2] = result[:, k * CHUNK:(k + 1) * CHUNK]

    each_peer(lambda r: b1_copy(r, me).start())
    for m in range(MOST):
        prcv[MOST * me + m] = pbox[m, my_half, :, group_rows(me)]

    @pl.loop(1, N_DP)
    def _(r):
        b1_copy(r, source(r)).wait_recv()

    for t in range(TILES):
        prow[t % NBLK, t // NBLK] = prcv[place[t]]

    each_peer(lambda r: b2_copy(r, me).start())
    pin[my_half, :, :, group_rows(me)] = prow[pair_of(me, my_half)]

    @pl.loop(1, N_DP)
    def _(r):
        b2_copy(r, source(r)).wait_recv()

    for i in range(PER):
        c = PER * me + i
        lanes = slice(i * CHUNK, (i + 1) * CHUNK)
        pre_acts_o[:, lanes] = pin[(c % 4) // 2, 0, c % 2]
        pre_grads_o[:, lanes] = pin[(c % 4) // 2, 1, c % 2]

    @pl.loop(1, N_DP)
    def _(r):
        ra_copy(r, me).wait_send()
        fa_copy(r, me).wait_send()
        fg_copy(r, me).wait_send()
        f2_copy(r, me).wait_send()
        b1_copy(r, me).wait_send()
        b2_copy(r, me).wait_send()

        @pl.loop(0, PARTS)
        def _(m):
            rs_copy(m, r).wait_send()

    @pl.when(sec > 0)
    def _():
        @pl.loop(0, PARTS)
        def _(m):
            hop(m).wait_send()


def shards(acts, grad_top, weights_t, slopes, running, ns_counts, assignment):
    owners = assignment[0]
    tile_ids = jnp.arange(TILES, dtype=jnp.int32)
    matches = (owners[:, None] == owners[None, :]) & (tile_ids[None, :] < tile_ids[:, None])
    place = owners * MOST + jnp.sum(matches.astype(jnp.int32), axis=1)
    taken = place[None, :] == jnp.arange(PLACES, dtype=jnp.int32)[:, None]
    table = jnp.sum(jnp.where(taken, tile_ids[None, :] + 1, 0), axis=1) - 1
    vmem = pl.BlockSpec(memory_space=pltpu.VMEM)
    smem = pl.BlockSpec(memory_space=pltpu.SMEM)
    hbm = pl.BlockSpec(memory_space=pl.ANY)
    flat = jax.ShapeDtypeStruct((ROWS, WIDTH), BF16)
    dma = pltpu.SemaphoreType.DMA
    square = (BLOCK, BLOCK)
    backs, pre_acts, pre_grads, inverses = pl.pallas_call(
        kernel,
        out_shape=(flat, flat, flat, jax.ShapeDtypeStruct((MOST,) + square, BF16)),
        in_specs=[smem, smem, smem, hbm, hbm, hbm, hbm, hbm],
        out_specs=(vmem, vmem, vmem, vmem),
        scratch_shapes=[
            pltpu.VMEM((WIDTH, NBLK * BLOCK), BF16),
            pltpu.VMEM((TILES, SLICE, BLOCK), F32),
            pltpu.VMEM((ROWS, WIDTH), BF16),
            pltpu.VMEM((ROWS, WIDTH), BF16),
            pltpu.VMEM((TILES, SLICE, BLOCK), BF16),
            pltpu.VMEM((PLACES, SLICE, BLOCK), BF16),
            pltpu.VMEM((MOST,) + square, BF16),
            pltpu.VMEM((ROWS, WIDTH), BF16),
            pltpu.VMEM((PARTS, N_DP, LOT, WIDTH), BF16),
            pltpu.VMEM((PARTS, N_DP, LOT, WIDTH), BF16),
            pltpu.VMEM((2 * PER, ROWS, CHUNK), BF16),
            pltpu.VMEM((CHUNKS, GROUP, CHUNK), BF16),
            pltpu.VMEM((PLACES, 2, GROUP, CHUNK), BF16),
            pltpu.VMEM((MOST, 2, 2, ROWS, CHUNK), BF16),
            pltpu.VMEM((MOST, 2, 2, ROWS, CHUNK), BF16),
            pltpu.VMEM((PLACES, 2, GROUP, CHUNK), BF16),
            pltpu.VMEM((NBLK, 2, 2, GROUP, CHUNK), BF16),
            pltpu.VMEM((2, 2, 2, ROWS, CHUNK), BF16),
            pltpu.VMEM(square, F32),
            pltpu.VMEM(square, F32),
            pltpu.VMEM(square, BF16),
            pltpu.VMEM(square, BF16),
            pltpu.VMEM(square, BF16),
            pltpu.VMEM(square, BF16),
            dma((SIDE,)), dma((4,)), dma((PARTS,)), dma((PARTS,)),
            dma((PARTS, N_DP)), dma((PARTS, N_DP)), pltpu.SemaphoreType.REGULAR,
        ] + [dma((N_DP,))] * 12,
        compiler_params=pltpu.CompilerParams(
            collective_id=0, has_side_effects=True, vmem_limit_bytes=48 * 1024 * 1024),
        name="refresh",
    )(table, place, ns_counts[0], acts[0], grad_top, slopes[0], weights_t[0], running[0])
    return (backs[None], pre_acts[None], pre_grads[None], inverses[None, None])


def solution(mesh):
    in_specs = (
        P("section", None, "dp"),
        P(None, "dp"),
        P("section", "dp", None),
        P("section", None, "dp"),
        P("section", None, "dp", None),
        P("section", None),
        P("section", None),
    )
    out_specs = (
        P("section", None, "dp"),
        P("section", None, "dp"),
        P("section", None, "dp"),
        P("section", "dp", None, None, None),
    )
    return jax.shard_map(shards, mesh=mesh, in_specs=in_specs, out_specs=out_specs, check_vma=False)
```
